32 devices in a mesh: dp: 4 (over y, core), expert: 8 (over z, x).
Axes of the slice: x: 2, y: 2, z: 4, core: 2. Of those that a mesh axis runs over, the one named last changes fastest.
Arguments:
- tokens: bfloat16 [2048, 2048], P(('dp', 'expert')), may hold values from -6 to 6
- expert_ids: int32 [2048, 8], P(('dp', 'expert')), may hold values from 0 to 15, as said below
- gates: bfloat16 [2048, 8], P(('dp', 'expert')), may hold values from 0.049804688 to 0.59765625
- kept_token: int32 [4, 16, 384], P('dp', 'expert'), may hold values from 0 to 511, as said below
- kept_count: int32 [4, 16, 8], P('dp', 'expert'), may hold values from 0 to 48, as said below
- w_gate: bfloat16 [16, 2048, 768], P('expert', 'dp'), may hold values from -0.125 to 0.125
- w_up: bfloat16 [16, 2048, 768], P('expert', 'dp'), may hold values from -0.125 to 0.125
- w_down: bfloat16 [16, 768, 2048], P('expert', None, 'dp'), may hold values from -0.21875 to 0.21875
Outputs:
- moe_output: bfloat16 [2048, 2048], P(('dp', 'expert'))
The draws below stay inside these ranges and needn't reach their ends.
Inputs may be any that keep to these rules, and one draw needn't show every extreme that they name: `expert_ids`: each row names 8 different experts. `kept_token`: slots c * 48 to c * 48 + 47 of expert e hold tokens of source device c of the group (tokens c * 64 to c * 64 + 63). The first kept_count[a, e, c] of them are, in rising order, the first tokens of that device whose expert_ids row names e; the other slots hold arbitrary tokens of that device. kept_count[a, e, c] is the number of tokens of source device c naming e, capped at 48. In every data group some expert has all its counts equal to 48.
All inputs are finite; a program needn't handle non-finite values.
Results may differ from the reference program's by a relative error of at most 0.005.
Values may be sent and summed in bfloat16 or wider, within the bound.
A program may use at most 128 MiB of HBM per device.

```python
import math
import jax
import jax.numpy as jnp
from jax import lax

D = 2048
FF = 768
TOP = 8
TOK_DEV = 64
EXPERTS = 16
GROUP = 512
TOKENS = 2048
CAP_SRC = 48
CAP_E = 384
N_DP = 4
N_EXPERT = 8


def routing(key):
    key_base, key_pop, key_hot, key_fill = jax.random.split(key, 4)
    base = jax.random.randint(key_base, (N_DP, GROUP, EXPERTS), 0, 65536, dtype=jnp.int32)
    popular = jax.random.randint(key_pop, (N_DP, 1, EXPERTS), 0, 4, dtype=jnp.int32)
    hottest = jax.random.randint(key_hot, (N_DP, 1, 1), 0, EXPERTS, dtype=jnp.int32)
    numbers = jnp.arange(EXPERTS, dtype=jnp.int32)
    score = (base + popular * 16384 + (numbers == hottest).astype(jnp.int32) * 1048576) * EXPERTS + numbers
    unused, chosen = lax.top_k(score, TOP)
    chosen = chosen.astype(jnp.int32)
    names_it = jnp.any(chosen[:, :, :, None] == numbers, axis=2).astype(jnp.int32)
    names_it = names_it.reshape(N_DP, N_EXPERT, TOK_DEV, EXPERTS)
    order = jnp.cumsum(names_it, axis=2) - 1
    position = jnp.where((names_it == 1) & (order < CAP_SRC), order, CAP_SRC)
    counts = jnp.minimum(jnp.sum(names_it, axis=2), CAP_SRC)
    slot_nums = jnp.arange(CAP_SRC, dtype=jnp.int32)
    matches = (position[:, :, :, :, None] == slot_nums).astype(jnp.int32)
    local_tok = jnp.sum(matches * jnp.arange(TOK_DEV, dtype=jnp.int32)[:, None, None], axis=2)
    filler = jax.random.randint(key_fill, local_tok.shape, 0, TOK_DEV, dtype=jnp.int32)
    local_tok = jnp.where(slot_nums < counts[:, :, :, None], local_tok, filler)
    group_tok = local_tok + (jnp.arange(N_EXPERT, dtype=jnp.int32) * TOK_DEV)[None, :, None, None]
    kept = jnp.transpose(group_tok, (0, 2, 1, 3)).reshape(N_DP, EXPERTS, CAP_E)
    kept_counts = jnp.transpose(counts, (0, 2, 1))
    return (chosen.reshape(TOKENS, TOP), kept, kept_counts)


def draw_expert_ids(key, part):
    shared = routing(key)
    return shared[0]


def draw_kept_token(key, part):
    shared = routing(key)
    return shared[1]


def draw_kept_count(key, part):
    shared = routing(key)
    return shared[2]


def levels(own_key, extent, pieces, low, high):
    gain, own = 1.0, jax.random.fold_in(own_key, 6)
    for dim, blocks in pieces:
        draws = jnp.exp(jax.random.uniform(jax.random.fold_in(own, dim), (blocks,), jnp.float32, low / len(pieces), high / len(pieces)))
        gain = gain * jnp.repeat(draws, extent[dim] // blocks).reshape([-1 if axis == dim else 1 for axis in range(len(extent))])
    return gain


def scatter_about(rng, shape, width, reach, pieces=(), held_as=jnp.bfloat16):
    loudness = levels(rng, shape, pieces, -0.22, 0.18) if pieces else 1.0
    entries = jax.random.normal(rng, shape, jnp.float32) * width * loudness
    return jnp.minimum(jnp.maximum(entries, -reach), reach).astype(held_as)


def setup_inputs(seed: int = 0) -> dict:
    splits = jax.random.split(jax.random.key(seed), 9)
    return {
        "tokens": scatter_about(splits[0], (TOKENS, D), 1.0, 6.0, ((0, 32),)),
        "expert_ids": draw_expert_ids(jax.random.fold_in(splits[8], 71), 0),
        "gates": jnp.clip(jnp.exp(math.log(0.59765625) - 2.4849066 * jax.random.uniform(splits[2], (TOKENS, TOP), jnp.float32) ** levels(splits[2], (TOKENS, TOP), ((0, 32),), -0.2, 0.2)), 0.049804688, 0.59765625).astype(jnp.bfloat16),
        "kept_token": draw_kept_token(jax.random.fold_in(splits[8], 71), 0),
        "kept_count": draw_kept_count(jax.random.fold_in(splits[8], 71), 0),
        "w_gate": scatter_about(splits[5], (EXPERTS, D, FF), D ** -0.5, 0.125, ((0, 8), (1, 4))),
        "w_up": scatter_about(splits[6], (EXPERTS, D, FF), D ** -0.5, 0.125, ((0, 8), (1, 4))),
        "w_down": scatter_about(splits[7], (EXPERTS, FF, D), FF ** -0.5, 0.21875, ((0, 8), (2, 4))),
    }


def reference(tokens, expert_ids, gates, kept_token, kept_count, w_gate, w_up, w_down):
    grouped = tokens.reshape(N_DP, GROUP, D)
    chosen = expert_ids.reshape(N_DP, GROUP, TOP)
    gate_vals = gates.reshape(N_DP, GROUP, TOP)
    slot_ids = jnp.arange(CAP_E, dtype=jnp.int32)
    results = []
    for group_idx in range(N_DP):
        group_rows = grouped[group_idx]
        group_ids = chosen[group_idx]
        group_gates = gate_vals[group_idx]

        def one_expert(total, inputs):
            expert_num, wg_one, wu_one, wd_one, token_list, counts = inputs
            usable = (slot_ids % CAP_SRC) < counts[slot_ids // CAP_SRC]
            names_it = group_ids[token_list] == expert_num
            weight = jnp.sum(jnp.where(names_it, group_gates[token_list].astype(jnp.float32), 0.0), axis=1)
            weight = jnp.where(usable, weight, 0.0)
            token_rows = group_rows[token_list].astype(jnp.float32)
            gate_act = jnp.dot(token_rows, wg_one.astype(jnp.float32))
            up_act = jnp.dot(token_rows, wu_one.astype(jnp.float32))
            hidden = (jax.nn.silu(gate_act) * up_act).astype(jnp.bfloat16)
            hidden = lax.optimization_barrier(hidden).astype(jnp.float32)
            expert_out = jnp.dot(hidden, wd_one.astype(jnp.float32))
            total = total.at[token_list].add(weight[:, None] * expert_out)
            return total, None

        start_total = jnp.zeros((GROUP, D), jnp.float32)
        total, unused = lax.scan(one_expert, start_total, (jnp.arange(EXPERTS, dtype=jnp.int32), w_gate, w_up, w_down, kept_token[group_idx], kept_count[group_idx]))
        results.append(total.astype(jnp.bfloat16))
    return jnp.concatenate(results, axis=0)
```

```python
import functools

import jax
import jax.numpy as jnp
from jax import lax
from jax.experimental import pallas as pl
from jax.experimental.pallas import tpu as pltpu
from jax.sharding import PartitionSpec as P

LANES = 128
TILE = 256


def moe_kernel(
    peers, ext, wg, wu, wd, out,
    tok, full_g, full_u, full_d, acc_g, acc_u, hid, part, landed, scale,
    own_sem, peer_send, peer_recv, sib_send, sib_recv, fwd_send, fwd_recv,
    tok_send, tok_recv, out_send, out_recv,
):
    dp = lax.axis_index("dp")
    me = lax.axis_index("expert")
    across = lax.rem(dp + 2, 4)
    sib = dp + 1 - 2 * lax.rem(dp, 2)
    diag = lax.rem(sib + 2, 4)
    rows = ext.shape[0]
    depth = wg.shape[1]
    ff = wg.shape[2]
    mine = pl.ds(pl.multiple_of(me * rows, rows), rows)

    def target(step):
        return lax.rem(me + step, peers)

    def dev(d, e):
        return {"dp": d, "expert": e}

    barrier = pltpu.get_barrier_semaphore()
    pl.semaphore_signal(barrier, inc=1, device_id=dev(across, me), device_id_type=pl.DeviceIdType.MESH)
    pl.semaphore_signal(barrier, inc=1, device_id=dev(sib, me), device_id_type=pl.DeviceIdType.MESH)
    for step in range(1, peers):
        pl.semaphore_signal(barrier, inc=1, device_id=dev(dp, target(step)), device_id_type=pl.DeviceIdType.MESH)
    pl.semaphore_wait(barrier, peers + 1)

    def part_src(k):
        if k < 4:
            return (wg, wu)[k % 2].at[k // 2]
        return wd.at[:, :, pl.ds((k - 4) * TILE, TILE)]

    def part_dst(k, q):
        if k < 4:
            return (full_g, full_u)[k % 2].at[q, k // 2]
        return full_d.at[q, k - 4]

    n_parts = 6

    def remote(src, dst, s, r, device):
        return pltpu.make_async_remote_copy(
            src_ref=src, dst_ref=dst, send_sem=s, recv_sem=r,
            device_id=device, device_id_type=pl.DeviceIdType.MESH,
        )

    to_peer = [
        remote(part_src(k), part_dst(k, dp), peer_send.at[k], peer_recv.at[k], dev(across, me))
        for k in range(n_parts)
    ]
    to_sib = [
        remote(part_src(k), part_dst(k, dp), sib_send.at[k], sib_recv.at[k], dev(sib, me))
        for k in range(n_parts)
    ]
    forward = [
        remote(part_dst(k, across), part_dst(k, across), fwd_send.at[k], fwd_recv.at[k], dev(sib, me))
        for k in range(n_parts)
    ]
    local = [
        pltpu.make_async_copy(part_src(k), part_dst(k, dp), own_sem.at[k]) for k in range(n_parts)
    ]
    token_copies = [
        remote(ext, tok.at[mine], tok_send.at[s - 1], tok_recv.at[s - 1], dev(dp, target(s)))
        for s in range(1, peers)
    ]

    to_peer[0].start()
    to_peer[1].start()
    for c in token_copies:
        c.start()
    for c in local:
        c.start()
    for c in to_sib:
        c.start()
    tok[mine, :] = ext[...]

    def pass_on(k):
        to_peer[k].wait_recv()
        forward[k].start()
        if k + 2 < n_parts:
            to_peer[k + 2].start()

    def project(k, q, first):
        weight, total = ((full_g, acc_g), (full_u, acc_u))[k % 2]
        j = k // 2

        def tile(t, carry):
            cols = pl.ds(pl.multiple_of(t * TILE, TILE), TILE)
            new = jnp.dot(
                tok[:, pl.ds(pl.multiple_of(q * depth, depth), depth)],
                weight[q, j, :, cols],
                preferred_element_type=jnp.float32,
            )
            if first:
                total[j, :, cols] = new
            else:
                total[j, :, cols] += new
            return carry

        lax.fori_loop(0, ff // TILE, tile, 0)

    def activate(j):
        def tile(t, carry):
            cols = pl.ds(pl.multiple_of(t * TILE, TILE), TILE)
            v = acc_g[j, :, cols]
            hid[j, :, cols] = (v / (1.0 + jnp.exp(-v)) * acc_u[j, :, cols]).astype(jnp.bfloat16)
            return carry

        lax.fori_loop(0, ff // TILE, tile, 0)

    pass_on(0)
    for c in token_copies:
        c.wait_recv()
    width = 4 * depth
    table = tok[:, width:].astype(jnp.float32)
    lane = lax.broadcasted_iota(jnp.int32, table.shape, 1)
    for j in range(2):
        one = jnp.sum(jnp.where(lane == 2 * me + j, table, 0.0), axis=1, keepdims=True)
        scale[j] = jnp.broadcast_to(one, table.shape)
    for k in range(4):
        local[k].wait()
        project(k, dp, True)
    pass_on(1)
    for k in range(4):
        to_sib[k].wait_recv()
        project(k, sib, False)
    project(0, across, False)
    project(1, across, False)
    for k in (0, 1):
        forward[k].wait_recv()
        project(k, diag, False)
    activate(0)
    pass_on(2)
    project(2, across, False)
    forward[2].wait_recv()
    project(2, diag, False)
    pass_on(3)
    project(3, across, False)
    forward[3].wait_recv()
    project(3, diag, False)
    activate(1)

    sends = []

    def down(h, q, slot):
        start = pl.multiple_of(q * depth + h * TILE, TILE)
        cols = pl.ds(start, TILE)
        total = None
        for j in range(2):
            new = jnp.dot(hid[j], full_d[q, h, j], preferred_element_type=jnp.float32)
            new = new * jnp.concatenate([scale[j]] * (TILE // LANES), axis=1)
            total = new if total is None else total + new
        part[:, cols] = total.astype(jnp.bfloat16)
        for s in range(1, peers):
            to = target(s)
            copy = remote(
                part.at[pl.ds(pl.multiple_of(to * rows, rows), rows), cols],
                landed.at[s - 1, :, cols],
                out_send.at[slot, s - 1],
                out_recv.at[slot, s - 1],
                dev(dp, to),
            )
            copy.start()
            sends.append(copy)

    def finish(h, q, slot):
        cols = pl.ds(pl.multiple_of(q * depth + h * TILE, TILE), TILE)
        for copy in sends[slot * (peers - 1):(slot + 1) * (peers - 1)]:
            copy.wait_recv()
        total = part[mine, cols].astype(jnp.float32)
        for s in range(peers - 1):
            total += landed[s, :, cols].astype(jnp.float32)
        out[:, cols] = total.astype(jnp.bfloat16)

    order = []

    def step(h, q):
        down(h, q, len(order))
        order.append((h, q))

    local[4].wait()
    step(0, dp)
    local[5].wait()
    step(1, dp)
    to_sib[4].wait_recv()
    step(0, sib)
    to_sib[5].wait_recv()
    step(1, sib)
    pass_on(4)
    step(0, across)
    forward[4].wait_recv()
    step(0, diag)
    pass_on(5)
    step(1, across)
    forward[5].wait_recv()
    step(1, diag)
    for slot, (h, q) in enumerate(order):
        finish(h, q, slot)

    for c in to_peer + to_sib + forward + token_copies + sends:
        c.wait_send()


def fits(n_dp, peers, tok_dev, width, per_device, ff):
    group = tok_dev * peers
    size = 3 * per_device * width * ff * 2 + group * (width + LANES) * 2
    size += per_device * group * ff * 10 + 2 * group * width * 2 + per_device * group * LANES * 4
    return (
        n_dp == 4 and per_device == 2 and per_device * peers <= LANES and ff % TILE == 0
        and width == 4 * 2 * TILE and tok_dev % 16 == 0 and size <= 44 * 2**20
    )


def fused(tokens, expert_ids, gates, cap_src, w_gate, w_up, w_down):
    peers = lax.axis_size("expert")
    rows, width = tokens.shape
    per_device, depth, ff = w_gate.shape
    group = rows * peers
    numbers = jnp.arange(LANES, dtype=jnp.int32)
    names = expert_ids[:, :, None] == numbers
    value = jnp.sum(jnp.where(names, gates.astype(jnp.float32)[:, :, None], 0.0), axis=1)
    named = jnp.any(names, axis=1).astype(jnp.bfloat16)
    place = jnp.arange(rows, dtype=jnp.int32)
    before = (place[:, None] >= place[None, :]).astype(jnp.bfloat16)
    rank = jnp.dot(before, named, preferred_element_type=jnp.float32)
    table = jnp.where(rank <= cap_src, value, 0.0).astype(jnp.bfloat16)
    ext = jnp.concatenate([tokens, table], axis=1)
    dma = pltpu.SemaphoreType.DMA
    n_down = width // TILE
    return pl.pallas_call(
        functools.partial(moe_kernel, peers),
        out_shape=jax.ShapeDtypeStruct((rows, width), jnp.bfloat16),
        in_specs=[pl.BlockSpec(memory_space=pltpu.VMEM)] + [pl.BlockSpec(memory_space=pl.ANY)] * 3,
        out_specs=pl.BlockSpec(memory_space=pltpu.VMEM),
        scratch_shapes=[
            pltpu.VMEM((group, width + LANES), jnp.bfloat16),
            pltpu.VMEM((4, per_device, depth, ff), jnp.bfloat16),
            pltpu.VMEM((4, per_device, depth, ff), jnp.bfloat16),
            pltpu.VMEM((4, depth // TILE, per_device, ff, TILE), jnp.bfloat16),
            pltpu.VMEM((per_device, group, ff), jnp.float32),
            pltpu.VMEM((per_device, group, ff), jnp.float32),
            pltpu.VMEM((per_device, group, ff), jnp.bfloat16),
            pltpu.VMEM((group, width), jnp.bfloat16),
            pltpu.VMEM((peers - 1, rows, width), jnp.bfloat16),
            pltpu.VMEM((per_device, group, LANES), jnp.float32),
            dma((6,)), dma((6,)), dma((6,)), dma((6,)), dma((6,)), dma((6,)), dma((6,)),
            dma((peers - 1,)), dma((peers - 1,)),
            dma((n_down, peers - 1)), dma((n_down, peers - 1)),
        ],
        compiler_params=pltpu.CompilerParams(
            collective_id=0, has_side_effects=True, vmem_limit_bytes=52 * 2**20
        ),
    )(ext, w_gate, w_up, w_down)


def expert_ffn(token_rows, w_gate, w_up, w_down):
    gate_new = jnp.einsum(
        "ecd,edf->ecf",
        token_rows,
        lax.all_gather(w_gate, "dp", axis=1, tiled=True),
        preferred_element_type=jnp.float32,
    )
    up_new = jnp.einsum(
        "ecd,edf->ecf",
        token_rows,
        lax.all_gather(w_up, "dp", axis=1, tiled=True),
        preferred_element_type=jnp.float32,
    )
    hidden = (jax.nn.silu(gate_new) * up_new).astype(jnp.bfloat16)
    return jnp.einsum(
        "ecf,efd->ecd",
        hidden,
        lax.all_gather(w_down, "dp", axis=2, tiled=True),
        preferred_element_type=jnp.float32,
    )


def body(tokens, expert_ids, gates, kept_token, kept_count, w_gate, w_up, w_down):
    my_rank = lax.axis_index("expert")
    peers = lax.axis_size("expert")
    per_device = w_gate.shape[0]
    tok_dev = tokens.shape[0]
    width = tokens.shape[1]
    top_count = expert_ids.shape[1]
    slot_list = kept_token[0]
    counts = kept_count[0]
    cap_e = slot_list.shape[1]
    cap_src = cap_e // peers
    group_size = tok_dev * peers
    if fits(lax.axis_size("dp"), peers, tok_dev, width, per_device, w_gate.shape[2]):
        return fused(tokens, expert_ids, gates, cap_src, w_gate, w_up, w_down)
    mine = my_rank * per_device + jnp.arange(per_device, dtype=jnp.int32)
    usable = (jnp.arange(cap_e, dtype=jnp.int32) % cap_src)[None, :] < jnp.repeat(
        counts, cap_src, axis=1
    )
    start_bufs = (
        jnp.zeros((group_size, width), jnp.bfloat16),
        jnp.zeros((group_size, top_count), jnp.int32),
        jnp.zeros((group_size, top_count), jnp.bfloat16),
    )
    pieces = (
        lax.all_gather(tokens, "expert", axis=0, tiled=True),
        lax.all_gather(expert_ids, "expert", axis=0, tiled=True),
        lax.all_gather(gates, "expert", axis=0, tiled=True),
    )
    first_row = jnp.int32(0)
    group_rows, group_ids, group_gates = tuple(
        (lax.dynamic_update_slice_in_dim(start_bufs[i], pieces[i], first_row, 0) for i in range(3))
    )
    token_rows = group_rows[slot_list]
    names_it = group_ids[slot_list] == mine[:, None, None]
    slot_weight = jnp.sum(
        jnp.where(names_it, group_gates[slot_list].astype(jnp.float32), 0.0), axis=2
    )
    slot_weight = jnp.where(usable, slot_weight, 0.0)
    outputs = expert_ffn(token_rows, w_gate, w_up, w_down)
    flat_out = (outputs * slot_weight[:, :, None]).reshape(-1, width)
    summed_all = jnp.zeros((group_size, width), jnp.float32).at[slot_list.reshape(-1)].add(flat_out)
    return lax.psum_scatter(summed_all, "expert", scatter_dimension=0, tiled=True).astype(
        jnp.bfloat16
    )


def solution(mesh):
    return jax.shard_map(
        body,
        mesh=mesh,
        in_specs=(
            P(("dp", "expert"), None),
            P(("dp", "expert"), None),
            P(("dp", "expert"), None),
            P("dp", "expert", None),
            P("dp", "expert", None),
            P("expert", "dp", None),
            P("expert", "dp", None),
            P("expert", None, "dp"),
        ),
        out_specs=P(("dp", "expert"), None),
        check_vma=False,
    )
```

```python
import functools

import jax
import jax.numpy as jnp
from jax import lax
from jax.experimental import pallas as pl
from jax.experimental.pallas import tpu as pltpu
from jax.sharding import PartitionSpec as P

LANES = 128
TILE = 256


def moe_kernel(
    peers, cap_src, tokens, ids, gates, wg, wu, wd, out,
    tok, full_g, full_u, full_d, acc_g, acc_u, hid, part, near, paired, landed, scale,
    own_sem, peer_send, peer_recv, sib_send, sib_recv, fwd_send, fwd_recv,
    tok_send, tok_recv, near_send, near_recv, line_send, line_recv, out_send, out_recv,
):
    dp = lax.axis_index("dp")
    me = lax.axis_index("expert")
    across = lax.rem(dp + 2, 4)
    sib = dp + 1 - 2 * lax.rem(dp, 2)
    diag = lax.rem(sib + 2, 4)
    rows, width = tokens.shape
    depth = wg.shape[1]
    ff = wg.shape[2]
    line = peers // 2
    side = lax.rem(me, 2)
    place = lax.div(me, 2)
    mine = pl.ds(pl.multiple_of(me * rows, rows), rows)
    home = pl.ds(pl.multiple_of(place * rows, rows), rows)

    def dev(d, e):
        return {"dp": d, "expert": e}

    def remote(src, dst, s, r, device):
        return pltpu.make_async_remote_copy(
            src_ref=src, dst_ref=dst, send_sem=s, recv_sem=r,
            device_id=device, device_id_type=pl.DeviceIdType.MESH,
        )

    def target(step):
        return lax.rem(me + step, peers)

    barrier = pltpu.get_barrier_semaphore()
    greeted = [dev(across, me), dev(sib, me)] + [dev(dp, target(s)) for s in range(1, peers)]
    for device in greeted:
        pl.semaphore_signal(barrier, inc=1, device_id=device, device_id_type=pl.DeviceIdType.MESH)
    pl.semaphore_wait(barrier, peers + 1)

    n_down = depth // LANES
    n_parts = 4 + n_down

    def part_src(k):
        if k < 4:
            return (wg, wu)[k % 2].at[k // 2]
        return wd.at[:, :, pl.ds((k - 4) * LANES, LANES)]

    def part_dst(k, q):
        if k < 4:
            return (full_g, full_u)[k % 2].at[q, k // 2]
        return full_d.at[q, :, :, pl.ds((k - 4) * LANES, LANES)]

    to_peer = [
        remote(part_src(k), part_dst(k, dp), peer_send.at[k], peer_recv.at[k], dev(across, me))
        for k in range(n_parts)
    ]
    forward = [
        remote(part_dst(k, across), part_dst(k, across), fwd_send.at[k], fwd_recv.at[k], dev(sib, me))
        for k in range(n_parts)
    ]
    whole = ((wg, full_g), (wu, full_u), (wd, full_d))
    to_sib = [
        remote(a, b.at[dp], sib_send.at[i], sib_recv.at[i], dev(sib, me))
        for i, (a, b) in enumerate(whole)
    ]
    local = [pltpu.make_async_copy(a, b.at[dp], own_sem.at[i]) for i, (a, b) in enumerate(whole)]
    token_copies = [
        remote(tok.at[mine], tok.at[mine], tok_send.at[s - 1], tok_recv.at[s - 1], dev(dp, target(s)))
        for s in range(1, peers)
    ]

    AHEAD = 3
    for k in range(AHEAD):
        to_peer[k].start()
    tok[mine, :width] = tokens[...]
    gate_vals = gates[...].astype(jnp.float32)
    chosen = ids[...]
    number = lax.broadcasted_iota(jnp.int32, (LANES, rows), 0)
    value = jnp.zeros((LANES, rows), jnp.float32)
    named = jnp.zeros((LANES, rows), jnp.float32)
    for k in range(chosen.shape[0]):
        hit = number == chosen[k:k + 1, :]
        value += jnp.where(hit, gate_vals[k:k + 1, :], 0.0)
        named += jnp.where(hit, 1.0, 0.0)
    first = lax.broadcasted_iota(jnp.int32, (rows, rows), 0)
    second = lax.broadcasted_iota(jnp.int32, (rows, rows), 1)
    upto = jnp.where(first <= second, 1.0, 0.0).astype(jnp.bfloat16)
    unit = jnp.where(first == second, 1.0, 0.0).astype(jnp.bfloat16)
    rank = jnp.dot(named.astype(jnp.bfloat16), upto, preferred_element_type=jnp.float32)
    kept = jnp.where(rank <= cap_src, value, 0.0).astype(jnp.bfloat16)
    tok[mine, width:] = lax.dot_general(
        unit, kept, (((1,), (1,)), ((), ())), preferred_element_type=jnp.float32
    ).astype(jnp.bfloat16)
    for c in token_copies:
        c.start()
    for c in local:
        c.start()
    for c in to_sib:
        c.start()

    def pass_on(k):
        to_peer[k].wait_recv()
        forward[k].start()
        if k + AHEAD < n_parts:
            to_peer[k + AHEAD].start()

    def project(k, q, first):
        weight, total = ((full_g, acc_g), (full_u, acc_u))[k % 2]
        j = k // 2

        def tile(t, carry):
            cols = pl.ds(pl.multiple_of(t * TILE, TILE), TILE)
            new = jnp.dot(
                tok[:, pl.ds(pl.multiple_of(q * depth, depth), depth)],
                weight[q, j, :, cols],
                preferred_element_type=jnp.float32,
            )
            if first:
                total[j, :, cols] = new
            else:
                total[j, :, cols] += new
            return carry

        lax.fori_loop(0, ff // TILE, tile, 0)

    def activate(j):
        def tile(t, carry):
            cols = pl.ds(pl.multiple_of(t * TILE, TILE), TILE)
            v = acc_g[j, :, cols]
            hid[j, :, cols] = (v / (1.0 + jnp.exp(-v)) * acc_u[j, :, cols]).astype(jnp.bfloat16)
            return carry

        lax.fori_loop(0, ff // TILE, tile, 0)

    pass_on(0)
    for c in token_copies:
        c.wait_recv()
    pass_on(1)
    table = tok[:, width:].astype(jnp.float32)
    lane = lax.broadcasted_iota(jnp.int32, table.shape, 1)
    for j in range(2):
        one = jnp.sum(jnp.where(lane == 2 * me + j, table, 0.0), axis=1, keepdims=True)
        scale[j] = jnp.broadcast_to(one, table.shape)
    for m in range(2):
        local[m].wait()
        project(m, dp, True)
        project(m + 2, dp, True)
    for m in range(2):
        to_sib[m].wait_recv()
        project(m, sib, False)
        project(m + 2, sib, False)
    for k in (0, 1):
        project(k, across, False)
    for k in (0, 1):
        forward[k].wait_recv()
        project(k, diag, False)
    pass_on(2)
    activate(0)
    project(2, across, False)
    forward[2].wait_recv()
    project(2, diag, False)
    pass_on(3)
    project(3, across, False)
    forward[3].wait_recv()
    project(3, diag, False)
    activate(1)

    def down(q, at, size):
        cols = pl.ds(pl.multiple_of(q * depth + at, size), size)
        total = None
        for j in range(2):
            new = jnp.dot(
                hid[j], full_d[q, j, :, pl.ds(at, size)], preferred_element_type=jnp.float32
            )
            new = new * jnp.concatenate([scale[j]] * (size // LANES), axis=1)
            total = new if total is None else total + new
        total = total.astype(jnp.bfloat16)
        for e in range(peers):
            part[e % 2, (e // 2) * rows:(e // 2 + 1) * rows, cols] = total[e * rows:(e + 1) * rows]
        return cols

    pairs, lines, direct = [], [], []

    def near_step(q, at):
        slot = len(pairs)
        cols = down(q, at, TILE)
        copy = remote(
            part.at[1 - side, :, cols], near.at[:, cols],
            near_send.at[slot], near_recv.at[slot], dev(dp, me + 1 - 2 * side),
        )
        copy.start()
        pairs.append((copy, cols))

    def line_step(slot):
        copy, cols = pairs[slot]
        copy.wait_recv()
        both = part[side, :, cols].astype(jnp.float32) + near[:, cols].astype(jnp.float32)
        paired[:, cols] = both.astype(jnp.bfloat16)
        sent = []
        for s in range(1, line):
            to = lax.rem(place + s, line)
            send = remote(
                paired.at[pl.ds(pl.multiple_of(to * rows, rows), rows), cols],
                landed.at[s - 1, :, cols],
                line_send.at[slot, s - 1], line_recv.at[slot, s - 1], dev(dp, 2 * to + side),
            )
            send.start()
            sent.append(send)
        lines.append(sent)

    def direct_step(q, at):
        slot = len(direct)
        cols = down(q, at, LANES)
        sent = []
        for s in range(1, peers):
            to = target(s)
            send = remote(
                part.at[lax.rem(to, 2), pl.ds(pl.multiple_of(lax.div(to, 2) * rows, rows), rows), cols],
                landed.at[s - 1, :, cols],
                out_send.at[slot, s - 1], out_recv.at[slot, s - 1], dev(dp, to),
            )
            send.start()
            sent.append(send)
        direct.append((sent, cols))

    def finish(sent, cols, own):
        for send in sent:
            send.wait_recv()
        total = own.astype(jnp.float32)
        for s in range(len(sent)):
            total += landed[s, :, cols].astype(jnp.float32)
        out[:, cols] = total.astype(jnp.bfloat16)

    def finish_line(slot):
        cols = pairs[slot][1]
        finish(lines[slot], cols, paired[home, cols])

    def finish_direct(slot):
        sent, cols = direct[slot]
        finish(sent, cols, part[side, home, cols])

    local[2].wait()
    near_step(dp, 0)
    near_step(dp, TILE)
    to_sib[2].wait_recv()
    near_step(sib, 0)
    near_step(sib, TILE)
    line_step(0)
    line_step(1)
    for c in range(n_down):
        pass_on(4 + c)
        if c == 0:
            line_step(2)
            line_step(3)
        direct_step(across, c * LANES)
        forward[4 + c].wait_recv()
        direct_step(diag, c * LANES)
        if c == 1:
            for slot in range(4):
                finish_line(slot)
        if c == 2:
            finish_direct(0)
            finish_direct(1)
    for slot in range(2, 2 * n_down):
        finish_direct(slot)

    for c in to_peer + to_sib + forward + token_copies:
        c.wait_send()
    for copy, unused in pairs:
        copy.wait_send()
    for sent in lines + [d[0] for d in direct]:
        for send in sent:
            send.wait_send()


def fits(n_dp, peers, tok_dev, width, per_device, ff):
    group = tok_dev * peers
    size = 3 * per_device * width * ff * 2 + group * (width + LANES) * 2
    size += per_device * group * ff * 10 + 3 * group * width * 2 + per_device * group * LANES * 4
    return (
        n_dp == 4 and per_device == 2 and per_device * peers <= LANES and ff % TILE == 0
        and width == 4 * 2 * TILE and tok_dev % 16 == 0 and tok_dev <= LANES
        and peers % 2 == 0 and peers >= 4 and size <= 46 * 2**20
    )


def fused(tokens, expert_ids, gates, cap_src, w_gate, w_up, w_down):
    peers = lax.axis_size("expert")
    rows, width = tokens.shape
    per_device, depth, ff = w_gate.shape
    group = rows * peers
    dma = pltpu.SemaphoreType.DMA
    n_parts = 4 + depth // LANES
    vmem = pl.BlockSpec(memory_space=pltpu.VMEM)
    return pl.pallas_call(
        functools.partial(moe_kernel, peers, cap_src),
        out_shape=jax.ShapeDtypeStruct((rows, width), jnp.bfloat16),
        in_specs=[vmem] * 3 + [pl.BlockSpec(memory_space=pl.ANY)] * 3,
        out_specs=vmem,
        scratch_shapes=[
            pltpu.VMEM((group, width + LANES), jnp.bfloat16),
            pltpu.VMEM((4, per_device, depth, ff), jnp.bfloat16),
            pltpu.VMEM((4, per_device, depth, ff), jnp.bfloat16),
            pltpu.VMEM((4, per_device, ff, depth), jnp.bfloat16),
            pltpu.VMEM((per_device, group, ff), jnp.float32),
            pltpu.VMEM((per_device, group, ff), jnp.float32),
            pltpu.VMEM((per_device, group, ff), jnp.bfloat16),
            pltpu.VMEM((2, group // 2, width), jnp.bfloat16),
            pltpu.VMEM((group // 2, width), jnp.bfloat16),
            pltpu.VMEM((group // 2, width), jnp.bfloat16),
            pltpu.VMEM((peers - 1, rows, width), jnp.bfloat16),
            pltpu.VMEM((per_device, group, LANES), jnp.float32),
            dma((3,)), dma((n_parts,)), dma((n_parts,)), dma((3,)), dma((3,)),
            dma((n_parts,)), dma((n_parts,)),
            dma((peers - 1,)), dma((peers - 1,)),
            dma((4,)), dma((4,)),
            dma((4, peers // 2 - 1)), dma((4, peers // 2 - 1)),
            dma((2 * (depth // LANES), peers - 1)), dma((2 * (depth // LANES), peers - 1)),
        ],
        compiler_params=pltpu.CompilerParams(
            collective_id=0, has_side_effects=True, vmem_limit_bytes=54 * 2**20
        ),
    )(tokens, expert_ids.T, gates.T, w_gate, w_up, w_down)


def expert_ffn(token_rows, w_gate, w_up, w_down):
    gate_new = jnp.einsum(
        "ecd,edf->ecf",
        token_rows,
        lax.all_gather(w_gate, "dp", axis=1, tiled=True),
        preferred_element_type=jnp.float32,
    )
    up_new = jnp.einsum(
        "ecd,edf->ecf",
        token_rows,
        lax.all_gather(w_up, "dp", axis=1, tiled=True),
        preferred_element_type=jnp.float32,
    )
    hidden = (jax.nn.silu(gate_new) * up_new).astype(jnp.bfloat16)
    return jnp.einsum(
        "ecf,efd->ecd",
        hidden,
        lax.all_gather(w_down, "dp", axis=2, tiled=True),
        preferred_element_type=jnp.float32,
    )


def body(tokens, expert_ids, gates, kept_token, kept_count, w_gate, w_up, w_down):
    my_rank = lax.axis_index("expert")
    peers = lax.axis_size("expert")
    per_device = w_gate.shape[0]
    tok_dev = tokens.shape[0]
    width = tokens.shape[1]
    top_count = expert_ids.shape[1]
    slot_list = kept_token[0]
    counts = kept_count[0]
    cap_e = slot_list.shape[1]
    cap_src = cap_e // peers
    group_size = tok_dev * peers
    if fits(lax.axis_size("dp"), peers, tok_dev, width, per_device, w_gate.shape[2]):
        return fused(tokens, expert_ids, gates, cap_src, w_gate, w_up, w_down)
    mine = my_rank * per_device + jnp.arange(per_device, dtype=jnp.int32)
    usable = (jnp.arange(cap_e, dtype=jnp.int32) % cap_src)[None, :] < jnp.repeat(
        counts, cap_src, axis=1
    )
    start_bufs = (
        jnp.zeros((group_size, width), jnp.bfloat16),
        jnp.zeros((group_size, top_count), jnp.int32),
        jnp.zeros((group_size, top_count), jnp.bfloat16),
    )
    pieces = (
        lax.all_gather(tokens, "expert", axis=0, tiled=True),
        lax.all_gather(expert_ids, "expert", axis=0, tiled=True),
        lax.all_gather(gates, "expert", axis=0, tiled=True),
    )
    first_row = jnp.int32(0)
    group_rows, group_ids, group_gates = tuple(
        (lax.dynamic_update_slice_in_dim(start_bufs[i], pieces[i], first_row, 0) for i in range(3))
    )
    token_rows = group_rows[slot_list]
    names_it = group_ids[slot_list] == mine[:, None, None]
    slot_weight = jnp.sum(
        jnp.where(names_it, group_gates[slot_list].astype(jnp.float32), 0.0), axis=2
    )
    slot_weight = jnp.where(usable, slot_weight, 0.0)
    outputs = expert_ffn(token_rows, w_gate, w_up, w_down)
    flat_out = (outputs * slot_weight[:, :, None]).reshape(-1, width)
    summed_all = jnp.zeros((group_size, width), jnp.float32).at[slot_list.reshape(-1)].add(flat_out)
    return lax.psum_scatter(summed_all, "expert", scatter_dimension=0, tiled=True).astype(
        jnp.bfloat16
    )


def solution(mesh):
    return jax.shard_map(
        body,
        mesh=mesh,
        in_specs=(
            P(("dp", "expert"), None),
            P(("dp", "expert"), None),
            P(("dp", "expert"), None),
            P("dp", "expert", None),
            P("dp", "expert", None),
            P("expert", "dp", None),
            P("expert", "dp", None),
            P("expert", None, "dp"),
        ),
        out_specs=P(("dp", "expert"), None),
        check_vma=False,
    )
```

```python
import functools

import jax
import jax.numpy as jnp
from jax import lax
from jax.experimental import pallas as pl
from jax.experimental.pallas import tpu as pltpu
from jax.sharding import PartitionSpec as P

LANES = 128
TILE = 256


def moe_kernel(
    peers, cap_src, tokens, ids, gates, wg, wu, wd, out,
    tok, full_g, full_u, full_d, acc_g, acc_u, hid, hid_out, part, near, paired, landed, scale,
    own_sem, peer_send, peer_recv, sib_send, sib_recv, fwd_send, fwd_recv,
    cross_send, cross_recv, tline_send, tline_recv, tpair_send, tpair_recv,
    near_send, near_recv, line_send, line_recv,
):
    dp = lax.axis_index("dp")
    me = lax.axis_index("expert")
    across = lax.rem(dp + 2, 4)
    sib = dp + 1 - 2 * lax.rem(dp, 2)
    diag = lax.rem(sib + 2, 4)
    rows, width = tokens.shape
    depth = wg.shape[1]
    ff = wg.shape[2]
    line = peers // 2
    side = lax.rem(me, 2)
    place = lax.div(me, 2)
    mine = pl.ds(pl.multiple_of(me * rows, rows), rows)
    level = lax.div(dp, 2)
    beside = me + 1 - 2 * side
    home = pl.ds(pl.multiple_of(place * rows, rows), rows)

    def dev(d, e):
        return {"dp": d, "expert": e}

    def remote(src, dst, s, r, device):
        return pltpu.make_async_remote_copy(
            src_ref=src, dst_ref=dst, send_sem=s, recv_sem=r,
            device_id=device, device_id_type=pl.DeviceIdType.MESH,
        )

    def along(step):
        return 2 * lax.rem(place + step, line) + side

    barrier = pltpu.get_barrier_semaphore()
    greeted = [dev(across, me), dev(sib, me), dev(dp, beside)]
    greeted += [dev(dp, along(s)) for s in range(1, line)]
    for device in greeted:
        pl.semaphore_signal(barrier, inc=1, device_id=device, device_id_type=pl.DeviceIdType.MESH)
    pl.semaphore_wait(barrier, len(greeted))

    n_down = depth // LANES
    n_parts = 2 + n_down

    def part_src(k):
        if k < 2:
            return (wg, wu)[k].at[1 - level]
        return wd.at[:, :, pl.ds((k - 2) * LANES, LANES)]

    def part_dst(k, q):
        if k < 2:
            return (full_g, full_u)[k].at[q]
        return full_d.at[q, :, :, pl.ds((k - 2) * LANES, LANES)]

    to_peer = [
        remote(part_src(k), part_dst(k, dp), peer_send.at[k], peer_recv.at[k], dev(across, me))
        for k in range(n_parts)
    ]
    forward = [
        remote(part_dst(k, across), part_dst(k, across), fwd_send.at[k], fwd_recv.at[k], dev(sib, me))
        for k in range(n_parts)
    ]
    whole = ((wg.at[level], full_g), (wu.at[level], full_u), (wd, full_d))
    to_sib = [
        remote(a, b.at[dp], sib_send.at[i], sib_recv.at[i], dev(sib, me))
        for i, (a, b) in enumerate(whole)
    ]
    local = [pltpu.make_async_copy(a, b.at[dp], own_sem.at[i]) for i, (a, b) in enumerate(whole)]
    def block(g, e):
        at = pl.ds(pl.multiple_of(e * rows, rows), rows)
        return tok.at[0, at] if g == 0 else tok.at[1, at, pl.ds(0, width)]

    token_over = remote(
        tokens, block(1, me), cross_send.at[0], cross_recv.at[0], dev(across, me)
    )
    hidden_over = remote(
        hid_out, hid.at[level], cross_send.at[1], cross_recv.at[1], dev(across, me)
    )
    token_line = [
        [
            remote(block(g, me), block(g, me), tline_send.at[g, s - 1], tline_recv.at[g, s - 1],
                   dev(dp, along(s)))
            for s in range(1, line)
        ]
        for g in range(2)
    ]
    token_pair = [
        [
            remote(block(g, along(line - s)), block(g, along(line - s)), tpair_send.at[g, s],
                   tpair_recv.at[g, s], dev(dp, beside))
            for s in range(line)
        ]
        for g in range(2)
    ]

    def spread(g):
        for c in token_line[g]:
            c.start()
        token_pair[g][0].start()

    def relay(g, s):
        token_line[g][s - 1].wait_recv()
        token_pair[g][s].start()

    AHEAD = 2
    token_over.start()
    for k in range(AHEAD):
        to_peer[k].start()
    tok[0, mine, :width] = tokens[...]
    gate_vals = gates[...].astype(jnp.float32)
    chosen = ids[...]
    number = lax.broadcasted_iota(jnp.int32, (LANES, rows), 0)
    value = jnp.zeros((LANES, rows), jnp.float32)
    named = jnp.zeros((LANES, rows), jnp.float32)
    for k in range(chosen.shape[0]):
        hit = number == chosen[k:k + 1, :]
        value += jnp.where(hit, gate_vals[k:k + 1, :], 0.0)
        named += jnp.where(hit, 1.0, 0.0)
    first = lax.broadcasted_iota(jnp.int32, (rows, rows), 0)
    second = lax.broadcasted_iota(jnp.int32, (rows, rows), 1)
    upto = jnp.where(first <= second, 1.0, 0.0).astype(jnp.bfloat16)
    unit = jnp.where(first == second, 1.0, 0.0).astype(jnp.bfloat16)
    rank = jnp.dot(named.astype(jnp.bfloat16), upto, preferred_element_type=jnp.float32)
    kept = jnp.where(rank <= cap_src, value, 0.0).astype(jnp.bfloat16)
    tok[0, mine, width:] = lax.dot_general(
        unit, kept, (((1,), (1,)), ((), ())), preferred_element_type=jnp.float32
    ).astype(jnp.bfloat16)
    for c in local:
        c.start()
    for c in to_sib:
        c.start()

    def pass_on(k):
        to_peer[k].wait_recv()
        forward[k].start()
        if k + AHEAD < n_parts:
            to_peer[k + AHEAD].start()

    def project(g, q, first):
        for weight, total in ((full_g, acc_g), (full_u, acc_u)):

            def tile(t, carry):
                cols = pl.ds(pl.multiple_of(t * TILE, TILE), TILE)
                new = jnp.dot(
                    tok[g, :, pl.ds(pl.multiple_of(q * depth, depth), depth)],
                    weight[q, :, cols],
                    preferred_element_type=jnp.float32,
                )
                if first:
                    total[:, cols] = new
                else:
                    total[:, cols] += new
                return carry

            lax.fori_loop(0, ff // TILE, tile, 0)

    def activate(store):
        def tile(t, carry):
            cols = pl.ds(pl.multiple_of(t * TILE, TILE), TILE)
            v = acc_g[:, cols]
            store(cols, (v / (1.0 + jnp.exp(-v)) * acc_u[:, cols]).astype(jnp.bfloat16))
            return carry

        lax.fori_loop(0, ff // TILE, tile, 0)

    def keep_out(cols, rows_out):
        hid_out[:, cols] = rows_out

    def keep_own(cols, rows_own):
        hid[level, :, cols] = rows_own

    token_over.wait_recv()
    spread(1)
    spread(0)
    pass_on(0)
    for s in range(1, line):
        relay(1, s)
    relay(0, 1)
    pass_on(1)
    for c in token_pair[1]:
        c.wait_recv()
    for m in range(2):
        local[m].wait()
    project(1, dp, True)
    for m in range(2):
        to_sib[m].wait_recv()
    project(1, sib, False)
    project(1, across, False)
    for k in range(2):
        forward[k].wait_recv()
    project(1, diag, False)
    activate(keep_out)
    hidden_over.start()
    for s in range(2, line):
        relay(0, s)
    pass_on(2)
    for c in token_pair[0]:
        c.wait_recv()
    for i, q in enumerate((dp, sib, across, diag)):
        project(0, q, i == 0)
    activate(keep_own)
    table = tok[0, :, width:].astype(jnp.float32)
    lane = lax.broadcasted_iota(jnp.int32, table.shape, 1)
    for j in range(2):
        one = jnp.sum(jnp.where(lane == 2 * me + j, table, 0.0), axis=1, keepdims=True)
        scale[j] = jnp.broadcast_to(one, table.shape)
    pass_on(3)
    hidden_over.wait_recv()

    def down(q, at, size):
        cols = pl.ds(pl.multiple_of(q * depth + at, size), size)
        total = None
        for j in range(2):
            new = jnp.dot(
                hid[j], full_d[q, j, :, pl.ds(at, size)], preferred_element_type=jnp.float32
            )
            new = new * jnp.concatenate([scale[j]] * (size // LANES), axis=1)
            total = new if total is None else total + new
        total = total.astype(jnp.bfloat16)
        for e in range(peers):
            part[e % 2, (e // 2) * rows:(e // 2 + 1) * rows, cols] = total[e * rows:(e + 1) * rows]
        return cols

    pairs, lines = [], []

    def near_step(q, at, size, lag):
        slot = len(pairs)
        cols = down(q, at, size)
        copy = remote(
            part.at[1 - side, :, cols], near.at[:, cols],
            near_send.at[slot], near_recv.at[slot], dev(dp, beside),
        )
        copy.start()
        pairs.append((copy, cols))
        flush(lag)

    def flush(lag):
        while len(pairs) - len(lines) > lag:
            line_step(len(lines))

    def line_step(slot):
        copy, cols = pairs[slot]
        copy.wait_recv()
        both = part[side, :, cols].astype(jnp.float32) + near[:, cols].astype(jnp.float32)
        paired[:, cols] = both.astype(jnp.bfloat16)
        sent = []
        for s in range(1, line):
            to = lax.rem(place + s, line)
            send = remote(
                paired.at[pl.ds(pl.multiple_of(to * rows, rows), rows), cols],
                landed.at[s - 1, :, cols],
                line_send.at[slot, s - 1], line_recv.at[slot, s - 1], dev(dp, 2 * to + side),
            )
            send.start()
            sent.append(send)
        lines.append(sent)

    def finish(sent, cols, own):
        for send in sent:
            send.wait_recv()
        total = own.astype(jnp.float32)
        for s in range(len(sent)):
            total += landed[s, :, cols].astype(jnp.float32)
        out[:, cols] = total.astype(jnp.bfloat16)

    def finish_line(slot):
        cols = pairs[slot][1]
        finish(lines[slot], cols, paired[home, cols])

    local[2].wait()
    near_step(dp, 0, TILE, 3)
    near_step(dp, TILE, TILE, 3)
    to_sib[2].wait_recv()
    near_step(sib, 0, TILE, 3)
    near_step(sib, TILE, TILE, 3)
    for c in range(n_down):
        if c == n_down - 1:
            flush(0)
            for slot in range(4):
                finish_line(slot)
        if c >= 2:
            pass_on(2 + c)
        near_step(across, c * LANES, LANES, 3)
        forward[2 + c].wait_recv()
        near_step(diag, c * LANES, LANES, 3)
    flush(0)
    for slot in range(4, len(pairs)):
        finish_line(slot)

    for c in to_peer + to_sib + forward + [token_over, hidden_over]:
        c.wait_send()
    for g in range(2):
        for c in token_line[g] + token_pair[g]:
            c.wait_send()
    for copy, unused in pairs:
        copy.wait_send()
    for sent in lines:
        for send in sent:
            send.wait_send()


def fits(n_dp, peers, tok_dev, width, per_device, ff):
    group = tok_dev * peers
    size = 3 * per_device * width * ff * 2 + group * (width + LANES) * 2
    size += per_device * group * ff * 10 + 3 * group * width * 2 + per_device * group * LANES * 4
    return (
        n_dp == 4 and per_device == 2 and per_device * peers <= LANES and ff % TILE == 0
        and width == 4 * 2 * TILE and tok_dev % 16 == 0 and tok_dev <= LANES
        and peers % 2 == 0 and peers >= 4 and size <= 46 * 2**20
    )


def fused(tokens, expert_ids, gates, cap_src, w_gate, w_up, w_down):
    peers = lax.axis_size("expert")
    rows, width = tokens.shape
    per_device, depth, ff = w_gate.shape
    group = rows * peers
    dma = pltpu.SemaphoreType.DMA
    n_parts = 2 + depth // LANES
    n_slots = 4 + 2 * (depth // LANES)
    line = peers // 2
    vmem = pl.BlockSpec(memory_space=pltpu.VMEM)
    return pl.pallas_call(
        functools.partial(moe_kernel, peers, cap_src),
        out_shape=jax.ShapeDtypeStruct((rows, width), jnp.bfloat16),
        in_specs=[vmem] * 3 + [pl.BlockSpec(memory_space=pl.ANY)] * 3,
        out_specs=vmem,
        scratch_shapes=[
            pltpu.VMEM((2, group, width + LANES), jnp.bfloat16),
            pltpu.VMEM((4, depth, ff), jnp.bfloat16),
            pltpu.VMEM((4, depth, ff), jnp.bfloat16),
            pltpu.VMEM((4, per_device, ff, depth), jnp.bfloat16),
            pltpu.VMEM((group, ff), jnp.float32),
            pltpu.VMEM((group, ff), jnp.float32),
            pltpu.VMEM((per_device, group, ff), jnp.bfloat16),
            pltpu.VMEM((group, ff), jnp.bfloat16),
            pltpu.VMEM((2, group // 2, width), jnp.bfloat16),
            pltpu.VMEM((group // 2, width), jnp.bfloat16),
            pltpu.VMEM((group // 2, width), jnp.bfloat16),
            pltpu.VMEM((line - 1, rows, width), jnp.bfloat16),
            pltpu.VMEM((per_device, group, LANES), jnp.float32),
            dma((3,)), dma((n_parts,)), dma((n_parts,)), dma((3,)), dma((3,)),
            dma((n_parts,)), dma((n_parts,)),
            dma((2,)), dma((2,)),
            dma((2, line - 1)), dma((2, line - 1)), dma((2, line)), dma((2, line)),
            dma((n_slots,)), dma((n_slots,)),
            dma((n_slots, line - 1)), dma((n_slots, line - 1)),
        ],
        compiler_params=pltpu.CompilerParams(
            collective_id=0, has_side_effects=True, vmem_limit_bytes=54 * 2**20
        ),
    )(tokens, expert_ids.T, gates.T, w_gate, w_up, w_down)


def expert_ffn(token_rows, w_gate, w_up, w_down):
    gate_new = jnp.einsum(
        "ecd,edf->ecf",
        token_rows,
        lax.all_gather(w_gate, "dp", axis=1, tiled=True),
        preferred_element_type=jnp.float32,
    )
    up_new = jnp.einsum(
        "ecd,edf->ecf",
        token_rows,
        lax.all_gather(w_up, "dp", axis=1, tiled=True),
        preferred_element_type=jnp.float32,
    )
    hidden = (jax.nn.silu(gate_new) * up_new).astype(jnp.bfloat16)
    return jnp.einsum(
        "ecf,efd->ecd",
        hidden,
        lax.all_gather(w_down, "dp", axis=2, tiled=True),
        preferred_element_type=jnp.float32,
    )


def body(tokens, expert_ids, gates, kept_token, kept_count, w_gate, w_up, w_down):
    my_rank = lax.axis_index("expert")
    peers = lax.axis_size("expert")
    per_device = w_gate.shape[0]
    tok_dev = tokens.shape[0]
    width = tokens.shape[1]
    top_count = expert_ids.shape[1]
    slot_list = kept_token[0]
    counts = kept_count[0]
    cap_e = slot_list.shape[1]
    cap_src = cap_e // peers
    group_size = tok_dev * peers
    if fits(lax.axis_size("dp"), peers, tok_dev, width, per_device, w_gate.shape[2]):
        return fused(tokens, expert_ids, gates, cap_src, w_gate, w_up, w_down)
    mine = my_rank * per_device + jnp.arange(per_device, dtype=jnp.int32)
    usable = (jnp.arange(cap_e, dtype=jnp.int32) % cap_src)[None, :] < jnp.repeat(
        counts, cap_src, axis=1
    )
    start_bufs = (
        jnp.zeros((group_size, width), jnp.bfloat16),
        jnp.zeros((group_size, top_count), jnp.int32),
        jnp.zeros((group_size, top_count), jnp.bfloat16),
    )
    pieces = (
        lax.all_gather(tokens, "expert", axis=0, tiled=True),
        lax.all_gather(expert_ids, "expert", axis=0, tiled=True),
        lax.all_gather(gates, "expert", axis=0, tiled=True),
    )
    first_row = jnp.int32(0)
    group_rows, group_ids, group_gates = tuple(
        (lax.dynamic_update_slice_in_dim(start_bufs[i], pieces[i], first_row, 0) for i in range(3))
    )
    token_rows = group_rows[slot_list]
    names_it = group_ids[slot_list] == mine[:, None, None]
    slot_weight = jnp.sum(
        jnp.where(names_it, group_gates[slot_list].astype(jnp.float32), 0.0), axis=2
    )
    slot_weight = jnp.where(usable, slot_weight, 0.0)
    outputs = expert_ffn(token_rows, w_gate, w_up, w_down)
    flat_out = (outputs * slot_weight[:, :, None]).reshape(-1, width)
    summed_all = jnp.zeros((group_size, width), jnp.float32).at[slot_list.reshape(-1)].add(flat_out)
    return lax.psum_scatter(summed_all, "expert", scatter_dimension=0, tiled=True).astype(
        jnp.bfloat16
    )


def solution(mesh):
    return jax.shard_map(
        body,
        mesh=mesh,
        in_specs=(
            P(("dp", "expert"), None),
            P(("dp", "expert"), None),
            P(("dp", "expert"), None),
            P("dp", "expert", None),
            P("dp", "expert", None),
            P("expert", "dp", None),
            P("expert", "dp", None),
            P("expert", None, "dp"),
        ),
        out_specs=P(("dp", "expert"), None),
        check_vma=False,
    )
```

```python
import functools

import jax
import jax.numpy as jnp
from jax import lax
from jax.experimental import pallas as pl
from jax.experimental.pallas import tpu as pltpu
from jax.sharding import PartitionSpec as P

LANES = 128
TILE = 256


def moe_kernel(
    peers, cap_src, tokens, ids, gates, wg, wu, wd, out,
    tok, full_g, full_u, full_d, acc_g, acc_u, hid, hid_out, part, near, paired, landed, scale,
    own_sem, peer_send, peer_recv, sib_send, sib_recv, fwd_send, fwd_recv,
    cross_send, cross_recv, tline_send, tline_recv, tpair_send, tpair_recv,
    near_send, near_recv, line_send, line_recv,
):
    dp = lax.axis_index("dp")
    me = lax.axis_index("expert")
    across = lax.rem(dp + 2, 4)
    sib = dp + 1 - 2 * lax.rem(dp, 2)
    diag = lax.rem(sib + 2, 4)
    rows, width = tokens.shape
    depth = wg.shape[1]
    ff = wg.shape[2]
    line = peers // 2
    side = lax.rem(me, 2)
    place = lax.div(me, 2)
    mine = pl.ds(pl.multiple_of(me * rows, rows), rows)
    level = lax.div(dp, 2)
    beside = me + 1 - 2 * side
    home = pl.ds(pl.multiple_of(place * rows, rows), rows)

    def dev(d, e):
        return {"dp": d, "expert": e}

    def remote(src, dst, s, r, device):
        return pltpu.make_async_remote_copy(
            src_ref=src, dst_ref=dst, send_sem=s, recv_sem=r,
            device_id=device, device_id_type=pl.DeviceIdType.MESH,
        )

    def along(step):
        return 2 * lax.rem(place + step, line) + side

    barrier = pltpu.get_barrier_semaphore()
    greeted = [dev(across, me), dev(sib, me), dev(dp, beside)]
    greeted += [dev(dp, along(s)) for s in range(1, line)]
    for device in greeted:
        pl.semaphore_signal(barrier, inc=1, device_id=device, device_id_type=pl.DeviceIdType.MESH)
    pl.semaphore_wait(barrier, len(greeted))

    n_down = depth // LANES
    n_parts = 2 + n_down

    def part_src(k):
        if k < 2:
            return (wg, wu)[k].at[1 - level]
        return wd.at[:, :, pl.ds((k - 2) * LANES, LANES)]

    def part_dst(k, q):
        if k < 2:
            return (full_g, full_u)[k].at[q]
        return full_d.at[q, :, :, pl.ds((k - 2) * LANES, LANES)]

    to_peer = [
        remote(part_src(k), part_dst(k, dp), peer_send.at[k], peer_recv.at[k], dev(across, me))
        for k in range(n_parts)
    ]
    forward = [
        remote(part_dst(k, across), part_dst(k, across), fwd_send.at[k], fwd_recv.at[k], dev(sib, me))
        for k in range(n_parts)
    ]
    whole = ((wg.at[level], full_g), (wu.at[level], full_u), (wd, full_d))
    to_sib = [
        remote(a, b.at[dp], sib_send.at[i], sib_recv.at[i], dev(sib, me))
        for i, (a, b) in enumerate(whole)
    ]
    local = [pltpu.make_async_copy(a, b.at[dp], own_sem.at[i]) for i, (a, b) in enumerate(whole)]
    def block(g, e):
        at = pl.ds(pl.multiple_of(e * rows, rows), rows)
        return tok.at[0, at] if g == 0 else tok.at[1, at, pl.ds(0, width)]

    token_over = remote(
        tokens, block(1, me), cross_send.at[0], cross_recv.at[0], dev(across, me)
    )
    hidden_over = remote(
        hid_out, hid.at[level], cross_send.at[1], cross_recv.at[1], dev(across, me)
    )
    token_line = [
        [
            remote(block(g, me), block(g, me), tline_send.at[g, s - 1], tline_recv.at[g, s - 1],
                   dev(dp, along(s)))
            for s in range(1, line)
        ]
        for g in range(2)
    ]
    token_pair = [
        [
            remote(block(g, along(line - s)), block(g, along(line - s)), tpair_send.at[g, s],
                   tpair_recv.at[g, s], dev(dp, beside))
            for s in range(line)
        ]
        for g in range(2)
    ]

    def spread(g):
        for c in token_line[g]:
            c.start()
        token_pair[g][0].start()

    def relay(g, s):
        token_line[g][s - 1].wait_recv()
        token_pair[g][s].start()

    AHEAD = 2
    token_over.start()
    for k in range(AHEAD):
        to_peer[k].start()
    tok[0, mine, :width] = tokens[...]
    gate_vals = gates[...].astype(jnp.float32)
    chosen = ids[...]
    number = lax.broadcasted_iota(jnp.int32, (LANES, rows), 0)
    value = jnp.zeros((LANES, rows), jnp.float32)
    named = jnp.zeros((LANES, rows), jnp.float32)
    for k in range(chosen.shape[0]):
        hit = number == chosen[k:k + 1, :]
        value += jnp.where(hit, gate_vals[k:k + 1, :], 0.0)
        named += jnp.where(hit, 1.0, 0.0)
    first = lax.broadcasted_iota(jnp.int32, (rows, rows), 0)
    second = lax.broadcasted_iota(jnp.int32, (rows, rows), 1)
    upto = jnp.where(first <= second, 1.0, 0.0).astype(jnp.bfloat16)
    unit = jnp.where(first == second, 1.0, 0.0).astype(jnp.bfloat16)
    rank = jnp.dot(named.astype(jnp.bfloat16), upto, preferred_element_type=jnp.float32)
    kept = jnp.where(rank <= cap_src, value, 0.0).astype(jnp.bfloat16)
    tok[0, mine, width:] = lax.dot_general(
        unit, kept, (((1,), (1,)), ((), ())), preferred_element_type=jnp.float32
    ).astype(jnp.bfloat16)
    for c in local:
        c.start()
    for c in to_sib:
        c.start()

    def pass_on(k):
        to_peer[k].wait_recv()
        forward[k].start()
        if k + AHEAD < n_parts:
            to_peer[k + AHEAD].start()

    def project(g, q, first):
        for weight, total in ((full_g, acc_g), (full_u, acc_u)):

            def tile(t, carry):
                cols = pl.ds(pl.multiple_of(t * TILE, TILE), TILE)
                new = jnp.dot(
                    tok[g, :, pl.ds(pl.multiple_of(q * depth, depth), depth)],
                    weight[q, :, cols],
                    preferred_element_type=jnp.float32,
                )
                if first:
                    total[:, cols] = new
                else:
                    total[:, cols] += new
                return carry

            lax.fori_loop(0, ff // TILE, tile, 0)

    def activate(store):
        def tile(t, carry):
            cols = pl.ds(pl.multiple_of(t * TILE, TILE), TILE)
            v = acc_g[:, cols]
            store(cols, (v / (1.0 + jnp.exp(-v)) * acc_u[:, cols]).astype(jnp.bfloat16))
            return carry

        lax.fori_loop(0, ff // TILE, tile, 0)

    def keep_out(cols, rows_out):
        hid_out[:, cols] = rows_out

    def keep_own(cols, rows_own):
        hid[level, :, cols] = rows_own

    token_over.wait_recv()
    spread(1)
    spread(0)
    pass_on(0)
    for s in range(1, line):
        relay(1, s)
    relay(0, 1)
    pass_on(1)
    for c in token_pair[1]:
        c.wait_recv()
    for m in range(2):
        local[m].wait()
    project(1, dp, True)
    for m in range(2):
        to_sib[m].wait_recv()
    project(1, sib, False)
    project(1, across, False)
    for k in range(2):
        forward[k].wait_recv()
    project(1, diag, False)
    activate(keep_out)
    hidden_over.start()
    for s in range(2, line):
        relay(0, s)
    pass_on(2)
    for c in token_pair[0]:
        c.wait_recv()
    for i, q in enumerate((dp, sib, across, diag)):
        project(0, q, i == 0)
    activate(keep_own)
    table = tok[0, :, width:].astype(jnp.float32)
    lane = lax.broadcasted_iota(jnp.int32, table.shape, 1)
    for j in range(2):
        one = jnp.sum(jnp.where(lane == 2 * me + j, table, 0.0), axis=1, keepdims=True)
        scale[j] = jnp.broadcast_to(one, table.shape)
    pass_on(3)
    hidden_over.wait_recv()

    def down(q, at, size):
        cols = pl.ds(pl.multiple_of(q * depth + at, size), size)
        total = None
        for j in range(2):
            new = jnp.dot(
                hid[j], full_d[q, j, :, pl.ds(at, size)], preferred_element_type=jnp.float32
            )
            new = new * jnp.concatenate([scale[j]] * (size // LANES), axis=1)
            total = new if total is None else total + new
        total = total.astype(jnp.bfloat16)
        for e in range(peers):
            part[e % 2, (e // 2) * rows:(e // 2 + 1) * rows, cols] = total[e * rows:(e + 1) * rows]
        return cols

    pairs, lines = [], []

    def near_step(q, at, size, lag):
        slot = len(pairs)
        cols = down(q, at, size)
        copy = remote(
            part.at[1 - side, :, cols], near.at[:, cols],
            near_send.at[slot], near_recv.at[slot], dev(dp, beside),
        )
        copy.start()
        pairs.append((copy, cols))
        flush(lag)

    def flush(lag):
        while len(pairs) - len(lines) > lag:
            line_step(len(lines))

    def line_step(slot):
        copy, cols = pairs[slot]
        copy.wait_recv()
        both = part[side, :, cols].astype(jnp.float32) + near[:, cols].astype(jnp.float32)
        paired[:, cols] = both.astype(jnp.bfloat16)
        sent = []
        for s in range(1, line):
            to = lax.rem(place + s, line)
            send = remote(
                paired.at[pl.ds(pl.multiple_of(to * rows, rows), rows), cols],
                landed.at[s - 1, :, cols],
                line_send.at[slot, s - 1], line_recv.at[slot, s - 1], dev(dp, 2 * to + side),
            )
            send.start()
            sent.append(send)
        lines.append(sent)

    def finish(sent, cols, own):
        for send in sent:
            send.wait_recv()
        total = own.astype(jnp.float32)
        for s in range(len(sent)):
            total += landed[s, :, cols].astype(jnp.float32)
        out[:, cols] = total.astype(jnp.bfloat16)

    def finish_line(slot):
        cols = pairs[slot][1]
        finish(lines[slot], cols, paired[home, cols])

    local[2].wait()
    near_step(dp, 0, TILE, 3)
    near_step(dp, TILE, TILE, 3)
    to_sib[2].wait_recv()
    near_step(sib, 0, TILE, 3)
    near_step(sib, TILE, TILE, 3)
    for c in range(n_down):
        if c >= 2:
            pass_on(2 + c)
        near_step(across, c * LANES, LANES, 3)
        forward[2 + c].wait_recv()
        near_step(diag, c * LANES, LANES, 3)
    flush(0)
    for slot in range(len(pairs)):
        finish_line(slot)

    for c in to_peer + to_sib + forward + [token_over, hidden_over]:
        c.wait_send()
    for g in range(2):
        for c in token_line[g] + token_pair[g]:
            c.wait_send()
    for copy, unused in pairs:
        copy.wait_send()
    for sent in lines:
        for send in sent:
            send.wait_send()


def fits(n_dp, peers, tok_dev, width, per_device, ff):
    group = tok_dev * peers
    size = 3 * per_device * width * ff * 2 + group * (width + LANES) * 2
    size += per_device * group * ff * 10 + 3 * group * width * 2 + per_device * group * LANES * 4
    return (
        n_dp == 4 and per_device == 2 and per_device * peers <= LANES and ff % TILE == 0
        and width == 4 * 2 * TILE and tok_dev % 16 == 0 and tok_dev <= LANES
        and peers % 2 == 0 and peers >= 4 and size <= 46 * 2**20
    )


def fused(tokens, expert_ids, gates, cap_src, w_gate, w_up, w_down):
    peers = lax.axis_size("expert")
    rows, width = tokens.shape
    per_device, depth, ff = w_gate.shape
    group = rows * peers
    dma = pltpu.SemaphoreType.DMA
    n_parts = 2 + depth // LANES
    n_slots = 4 + 2 * (depth // LANES)
    line = peers // 2
    vmem = pl.BlockSpec(memory_space=pltpu.VMEM)
    return pl.pallas_call(
        functools.partial(moe_kernel, peers, cap_src),
        out_shape=jax.ShapeDtypeStruct((rows, width), jnp.bfloat16),
        in_specs=[vmem] * 3 + [pl.BlockSpec(memory_space=pl.ANY)] * 3,
        out_specs=vmem,
        scratch_shapes=[
            pltpu.VMEM((2, group, width + LANES), jnp.bfloat16),
            pltpu.VMEM((4, depth, ff), jnp.bfloat16),
            pltpu.VMEM((4, depth, ff), jnp.bfloat16),
            pltpu.VMEM((4, per_device, ff, depth), jnp.bfloat16),
            pltpu.VMEM((group, ff), jnp.float32),
            pltpu.VMEM((group, ff), jnp.float32),
            pltpu.VMEM((per_device, group, ff), jnp.bfloat16),
            pltpu.VMEM((group, ff), jnp.bfloat16),
            pltpu.VMEM((2, group // 2, width), jnp.bfloat16),
            pltpu.VMEM((group // 2, width), jnp.bfloat16),
            pltpu.VMEM((group // 2, width), jnp.bfloat16),
            pltpu.VMEM((line - 1, rows, width), jnp.bfloat16),
            pltpu.VMEM((per_device, group, LANES), jnp.float32),
            dma((3,)), dma((n_parts,)), dma((n_parts,)), dma((3,)), dma((3,)),
            dma((n_parts,)), dma((n_parts,)),
            dma((2,)), dma((2,)),
            dma((2, line - 1)), dma((2, line - 1)), dma((2, line)), dma((2, line)),
            dma((n_slots,)), dma((n_slots,)),
            dma((n_slots, line - 1)), dma((n_slots, line - 1)),
        ],
        compiler_params=pltpu.CompilerParams(
            collective_id=0, has_side_effects=True, vmem_limit_bytes=54 * 2**20
        ),
    )(tokens, expert_ids.T, gates.T, w_gate, w_up, w_down)


def expert_ffn(token_rows, w_gate, w_up, w_down):
    gate_new = jnp.einsum(
        "ecd,edf->ecf",
        token_rows,
        lax.all_gather(w_gate, "dp", axis=1, tiled=True),
        preferred_element_type=jnp.float32,
    )
    up_new = jnp.einsum(
        "ecd,edf->ecf",
        token_rows,
        lax.all_gather(w_up, "dp", axis=1, tiled=True),
        preferred_element_type=jnp.float32,
    )
    hidden = (jax.nn.silu(gate_new) * up_new).astype(jnp.bfloat16)
    return jnp.einsum(
        "ecf,efd->ecd",
        hidden,
        lax.all_gather(w_down, "dp", axis=2, tiled=True),
        preferred_element_type=jnp.float32,
    )


def body(tokens, expert_ids, gates, kept_token, kept_count, w_gate, w_up, w_down):
    my_rank = lax.axis_index("expert")
    peers = lax.axis_size("expert")
    per_device = w_gate.shape[0]
    tok_dev = tokens.shape[0]
    width = tokens.shape[1]
    top_count = expert_ids.shape[1]
    slot_list = kept_token[0]
    counts = kept_count[0]
    cap_e = slot_list.shape[1]
    cap_src = cap_e // peers
    group_size = tok_dev * peers
    if fits(lax.axis_size("dp"), peers, tok_dev, width, per_device, w_gate.shape[2]):
        return fused(tokens, expert_ids, gates, cap_src, w_gate, w_up, w_down)
    mine = my_rank * per_device + jnp.arange(per_device, dtype=jnp.int32)
    usable = (jnp.arange(cap_e, dtype=jnp.int32) % cap_src)[None, :] < jnp.repeat(
        counts, cap_src, axis=1
    )
    start_bufs = (
        jnp.zeros((group_size, width), jnp.bfloat16),
        jnp.zeros((group_size, top_count), jnp.int32),
        jnp.zeros((group_size, top_count), jnp.bfloat16),
    )
    pieces = (
        lax.all_gather(tokens, "expert", axis=0, tiled=True),
        lax.all_gather(expert_ids, "expert", axis=0, tiled=True),
        lax.all_gather(gates, "expert", axis=0, tiled=True),
    )
    first_row = jnp.int32(0)
    group_rows, group_ids, group_gates = tuple(
        (lax.dynamic_update_slice_in_dim(start_bufs[i], pieces[i], first_row, 0) for i in range(3))
    )
    token_rows = group_rows[slot_list]
    names_it = group_ids[slot_list] == mine[:, None, None]
    slot_weight = jnp.sum(
        jnp.where(names_it, group_gates[slot_list].astype(jnp.float32), 0.0), axis=2
    )
    slot_weight = jnp.where(usable, slot_weight, 0.0)
    outputs = expert_ffn(token_rows, w_gate, w_up, w_down)
    flat_out = (outputs * slot_weight[:, :, None]).reshape(-1, width)
    summed_all = jnp.zeros((group_size, width), jnp.float32).at[slot_list.reshape(-1)].add(flat_out)
    return lax.psum_scatter(summed_all, "expert", scatter_dimension=0, tiled=True).astype(
        jnp.bfloat16
    )


def solution(mesh):
    return jax.shard_map(
        body,
        mesh=mesh,
        in_specs=(
            P(("dp", "expert"), None),
            P(("dp", "expert"), None),
            P(("dp", "expert"), None),
            P("dp", "expert", None),
            P("dp", "expert", None),
            P("expert", "dp", None),
            P("expert", "dp", None),
            P("expert", None, "dp"),
        ),
        out_specs=P(("dp", "expert"), None),
        check_vma=False,
    )
```
